32 devices in a mesh: layer: 4 (over x, core), proc: 8 (over z, y).
Axes of the slice: x: 2, y: 2, z: 4, core: 2. Of those that a mesh axis runs over, the one named last changes fastest.
Arguments:
- owner: int32 [4, 6], P('layer'), may hold values from 0 to 7
- rhs_blocks: bfloat16 [8192, 256], P(('layer', 'proc')), may hold values from -6 to 6
- chain_blocks: bfloat16 [8192, 256], P(('layer', 'proc')), may hold values from -0.1875 to 0.1875
- diag_inverse: bfloat16 [8192, 256], P(('layer', 'proc')), may hold values from -1 to 2
- factor_blocks: bfloat16 [655360, 256], P(('layer', 'proc')), may hold values from -0.015625 to 0.015625
- col_index: int32 [32, 80], P(('layer', 'proc')), may hold values from 0 to 5
- row_index: int32 [32, 80], P(('layer', 'proc')), may hold values from 0 to 3
- anc_rhs: float32 [1024, 256], P(None, 'proc'), may hold values from -6 to 6
- anc_inverse: bfloat16 [1024, 256], replicated, may hold values from -1 to 2
Outputs:
- solved: bfloat16 [6144, 256], P('layer', 'proc')
- ancestor: float32 [1024, 256], P(None, 'proc')
The draws below stay inside these ranges and needn't reach their ends.
All inputs are finite; a program needn't handle non-finite values.
Results may differ from the reference program's by a relative error of at most 0.006.
Values may be sent and summed in bfloat16 or wider, within the bound.
No kernel may reach another device: no remote copies, remote signals or barrier semaphores. Data moves between devices by JAX's collectives and lax.ppermute only.
A program may use at most 128 MiB of HBM per device.

```python
import math
import jax
import jax.numpy as jnp
from jax import lax

B = 256
R = 256
TICKS = 6
NBLK = 80
ABLK = 4
ANC = 1024
N_LAYER = 4
N_PROC = 8


def inverse_stack(key, count):
    noise = jax.random.truncated_normal(key, -4.0, 4.0, (count, B, B), jnp.float32)
    stacked = jnp.eye(B, dtype=jnp.float32)[None, :, :] + 0.5 * noise / math.sqrt(B)
    return stacked.reshape(count * B, B).astype(jnp.bfloat16)


def draw_diag_inverse(key, part):
    return inverse_stack(jax.random.fold_in(key, 11), N_LAYER * N_PROC)


def draw_anc_inverse(key, part):
    return inverse_stack(jax.random.fold_in(key, 23), ABLK)


def touch_ends(values, rng, smallest, largest):
    shape = values.shape
    spot = [jax.random.randint(jax.random.fold_in(rng, axis), (), 0, shape[axis]) for axis in range(len(shape))]
    values = values.at[tuple(spot)].set(smallest)
    longest = shape.index(max(shape))
    spot[longest] = (spot[longest] + 1) % shape[longest]
    return values.at[tuple(spot)].set(largest)


def shard_levels(stream_key, shape, split, least, high):
    factor_of, own = 1.0, jax.random.fold_in(stream_key, 6)
    for position, parts in split:
        draws = jnp.exp(jax.random.uniform(jax.random.fold_in(own, position), (parts,), jnp.float32, least / len(split), high / len(split)))
        factor_of = factor_of * jnp.repeat(draws, shape[position] // parts).reshape([-1 if axis == position else 1 for axis in range(len(shape))])
    return factor_of


def gaussian(own_key, extent, scale, most, split=(), kind=jnp.bfloat16):
    loudness = shard_levels(own_key, extent, split, -0.22, 0.18) if split else 1.0
    drawn = jax.random.normal(own_key, extent, jnp.float32) * scale * loudness
    return jnp.minimum(jnp.maximum(drawn, -most), most).astype(kind)


def setup_inputs(seed: int = 0) -> dict:
    keys = jax.random.split(jax.random.key(seed), 10)
    return {
        "owner": touch_ends(jax.random.randint(keys[0], (N_LAYER, TICKS), 0, N_PROC), jax.random.fold_in(keys[0], 1), 0, N_PROC - 1).astype(jnp.int32),
        "rhs_blocks": gaussian(keys[1], (N_LAYER * N_PROC * B, R), 1.0, 6.0, ((0, 32),)),
        "chain_blocks": gaussian(keys[2], (N_LAYER * N_PROC * B, B), (4 * B) ** -0.5, 0.1875, ((0, 32),)),
        "diag_inverse": draw_diag_inverse(jax.random.fold_in(keys[9], 71), 0),
        "factor_blocks": gaussian(keys[4], (N_LAYER * N_PROC * NBLK * B, B), (B * NBLK * N_LAYER * N_PROC // ABLK) ** -0.5, 0.015625, ((0, 32),)),
        "col_index": touch_ends(jax.random.randint(keys[5], (N_LAYER * N_PROC, NBLK), 0, TICKS), jax.random.fold_in(keys[5], 1), 0, TICKS - 1).astype(jnp.int32),
        "row_index": touch_ends(jax.random.randint(keys[6], (N_LAYER * N_PROC, NBLK), 0, ABLK), jax.random.fold_in(keys[6], 1), 0, ABLK - 1).astype(jnp.int32),
        "anc_rhs": gaussian(keys[7], (ANC, R), 1.0, 6.0, ((1, 8),), jnp.float32),
        "anc_inverse": draw_anc_inverse(jax.random.fold_in(keys[9], 71), 0),
    }


def accumulate(running, members):
    factor_set, col_set, row_set = members
    col_hot = (col_set[:, None] == jnp.arange(TICKS)[None, :]).astype(jnp.float32)
    row_hot = (row_set[:, None] == jnp.arange(ABLK)[None, :]).astype(jnp.float32)
    update = jnp.einsum("ka,kt,kbc->atbc", row_hot, col_hot, factor_set.astype(jnp.float32), precision=lax.Precision.HIGHEST)
    return running + update, None


def reference(owner, rhs_blocks, chain_blocks, diag_inverse, factor_blocks, col_index, row_index, anc_rhs, anc_inverse):
    rhs_all = rhs_blocks.reshape(N_LAYER * N_PROC, B, R)
    chain_all = chain_blocks.reshape(N_LAYER * N_PROC, B, B)
    inverse_all = diag_inverse.reshape(N_LAYER * N_PROC, B, B)
    factors = factor_blocks.reshape(N_LAYER, N_PROC * NBLK, B, B)
    col_layers = col_index.reshape(N_LAYER, N_PROC * NBLK)
    row_layers = row_index.reshape(N_LAYER, N_PROC * NBLK)
    summed = jnp.zeros((ABLK, B, R), jnp.float32)
    solved_layers = []
    for layer_index in range(N_LAYER):
        previous = jnp.zeros((B, R), jnp.bfloat16)
        solved_ticks = []
        for tick_index in range(TICKS):
            slot_index = layer_index * N_PROC + owner[layer_index, tick_index]
            reduced = rhs_all[slot_index].astype(jnp.float32) - jnp.dot(chain_all[slot_index], previous, preferred_element_type=jnp.float32)
            previous = jnp.dot(inverse_all[slot_index], reduced.astype(jnp.bfloat16), preferred_element_type=jnp.float32).astype(jnp.bfloat16)
            solved_ticks.append(previous)
        stacked = jnp.stack(solved_ticks)
        solved_layers.append(stacked)
        grouped, unused = lax.scan(accumulate, jnp.zeros((ABLK, TICKS, B, B), jnp.float32), (factors[layer_index].reshape(N_PROC, NBLK, B, B), col_layers[layer_index].reshape(N_PROC, NBLK), row_layers[layer_index].reshape(N_PROC, NBLK)))
        summed = summed + jnp.einsum("atbc,tcr->abr", grouped, stacked.astype(jnp.float32), precision=lax.Precision.HIGHEST)
    remaining = (anc_rhs - summed.reshape(ANC, R)).astype(jnp.bfloat16).reshape(ABLK, B, R)
    inverse = anc_inverse.reshape(ABLK, B, B)
    ancestor = jnp.einsum("abc,acr->abr", inverse.astype(jnp.float32), remaining.astype(jnp.float32), precision=lax.Precision.HIGHEST).reshape(ANC, R)
    solved = jnp.stack(solved_layers).reshape(N_LAYER * TICKS * B, R)
    return solved, ancestor
```

```python
import functools

import jax
import jax.numpy as jnp
from jax import lax
from jax.experimental import pallas as pl
from jax.experimental.pallas import tpu as pltpu
from jax.sharding import PartitionSpec as P

BF16 = jnp.bfloat16
F32 = jnp.float32
VMEM_LIMIT = 24 * 1024 * 1024
SMALL_LIMIT = 8 * 1024 * 1024
OPERATOR_LIMIT = 60 * 1024 * 1024
GROUP_LIMIT = 50 * 1024 * 1024


def vmem_spec():
    return pl.BlockSpec(memory_space=pltpu.VMEM)


def smem_spec():
    return pl.BlockSpec(memory_space=pltpu.SMEM)


def operator_kernel(diag_ref, chain_ref, rhs_ref, out_ref, diag, chain, rhs, arrived):
    copies = [
        pltpu.make_async_copy(source, target, arrived.at[i])
        for i, (source, target) in enumerate([(diag_ref, diag), (chain_ref, chain), (rhs_ref, rhs)])
    ]
    for copy in copies:
        copy.start()
    for copy in copies:
        copy.wait()
    block = chain.shape[1]
    out_ref[:block, :] = (-jnp.dot(diag[...], chain[...], preferred_element_type=F32)).T.astype(BF16)
    out_ref[block:, :] = jnp.dot(diag[...], rhs[...], preferred_element_type=F32).T.astype(BF16)


def operators(diag_inverse, chain_blocks, rhs_blocks):
    block = chain_blocks.shape[0]
    inputs = (diag_inverse, chain_blocks, rhs_blocks)
    return pl.pallas_call(
        operator_kernel,
        out_shape=jax.ShapeDtypeStruct((block + rhs_blocks.shape[1], block), BF16),
        in_specs=[pl.BlockSpec(memory_space=pl.ANY)] * 3,
        out_specs=vmem_spec(),
        scratch_shapes=[pltpu.VMEM(i.shape, BF16) for i in inputs] + [pltpu.SemaphoreType.DMA((3,))],
        compiler_params=pltpu.CompilerParams(vmem_limit_bytes=OPERATOR_LIMIT),
        name="operators",
    )(*inputs)


def group_kernel(ticks, anc_count, pair_ref, factor_ref, out_ref, total, held, arrived):
    block = total.shape[1]
    chunks = arrived.shape[0]
    per_chunk = held.shape[0] // (chunks * block)

    def fetch(i):
        rows = pl.ds(pl.multiple_of(i * per_chunk * block, block), per_chunk * block)
        return pltpu.make_async_copy(factor_ref.at[rows], held.at[rows], arrived.at[i])

    for i in range(chunks):
        fetch(i).start()
    total[...] = jnp.zeros_like(total)

    def add(i, carry):
        fetch(i).wait()
        for j in range(per_chunk):
            k = i * per_chunk + j
            total[pair_ref[k]] += held[pl.ds(pl.multiple_of(k * block, block), block), :].astype(F32)
        return carry

    lax.fori_loop(0, chunks, add, 0)
    for a in range(anc_count):
        for t in range(ticks):
            out_ref[t * block : (t + 1) * block, a * block : (a + 1) * block] = total[a * ticks + t].T.astype(BF16)


def grouped(pair, factor_blocks, ticks, anc_count):
    count = pair.shape[0]
    block = factor_blocks.shape[1]
    chunks = next(count // s for s in (8, 5, 4, 2, 1) if count % s == 0)
    return pl.pallas_call(
        functools.partial(group_kernel, ticks, anc_count),
        out_shape=jax.ShapeDtypeStruct((ticks * block, anc_count * block), BF16),
        in_specs=[smem_spec(), pl.BlockSpec(memory_space=pl.ANY)],
        out_specs=vmem_spec(),
        scratch_shapes=[
            pltpu.VMEM((anc_count * ticks, block, block), F32),
            pltpu.VMEM(factor_blocks.shape, BF16),
            pltpu.SemaphoreType.DMA((chunks,)),
        ],
        compiler_params=pltpu.CompilerParams(vmem_limit_bytes=GROUP_LIMIT),
        cost_estimate=pl.CostEstimate(flops=factor_blocks.size, bytes_accessed=2 * factor_blocks.size, transcendentals=0),
        name="grouped",
    )(pair, factor_blocks)


def solve_kernel(ticks, owner_ref, group_ref, *refs):
    operator_refs, (x_ref, send_ref, keep_ref, product) = refs[:-4], refs[-4:]
    proc, core = lax.axis_index("proc"), lax.axis_index("layer") % 2
    block = operator_refs[0].shape[1]
    half = send_ref.shape[1]
    places = [(ref.at[:block], ref.at[block:]) for ref in operator_refs]
    for j, (step_ref, start_ref) in enumerate(places):

        @pl.when(owner_ref[0, 0] ^ proc == j)
        def _(start_ref=start_ref):
            x_ref[:, :block] = start_ref[...]

    def tick(t, carry):
        before = pl.multiple_of((t - 1) * block, block)
        here = pl.multiple_of(t * block, block)
        previous = x_ref[:, pl.ds(before, block)]
        for j, (step_ref, start_ref) in enumerate(places):

            @pl.when(owner_ref[0, t] ^ proc == j)
            def _(step_ref=step_ref, start_ref=start_ref):
                value = start_ref[...].astype(F32) + jnp.dot(previous, step_ref[...], preferred_element_type=F32)
                x_ref[:, pl.ds(here, block)] = value.astype(BF16)

        return carry

    lax.fori_loop(1, ticks, tick, 0)
    product[...] = jnp.dot(x_ref[...], group_ref[...], preferred_element_type=F32)
    mine = pl.multiple_of(core * half, half)
    other = pl.multiple_of((1 - core) * half, half)
    keep_ref[...] = product[:, pl.ds(mine, half)]
    send_ref[...] = product[:, pl.ds(other, half)].astype(BF16)


def solve(owner, held, group):
    ticks = owner.shape[1]
    block = held[0].shape[1]
    rhs_width = held[0].shape[0] - block
    anc_rows = group.shape[1]
    return pl.pallas_call(
        functools.partial(solve_kernel, ticks),
        out_shape=(
            jax.ShapeDtypeStruct((rhs_width, ticks * block), BF16),
            jax.ShapeDtypeStruct((rhs_width, anc_rows // 2), BF16),
            jax.ShapeDtypeStruct((rhs_width, anc_rows // 2), F32),
        ),
        in_specs=[smem_spec()] + [vmem_spec()] * (1 + len(held)),
        out_specs=(vmem_spec(), vmem_spec(), vmem_spec()),
        scratch_shapes=[pltpu.VMEM((rhs_width, anc_rows), F32)],
        compiler_params=pltpu.CompilerParams(vmem_limit_bytes=VMEM_LIMIT),
        name="solve",
    )(owner, group, *held)


def ancestor_kernel(mine_ref, other_ref, inverse_ref, out_ref):
    block = inverse_ref.shape[1]
    half = mine_ref.shape[1]
    first = lax.axis_index("layer") % 2 == 0
    mine, other = mine_ref[...], other_ref[...]
    low, high = jnp.where(first, mine, other), jnp.where(first, other, mine)
    for a in range(inverse_ref.shape[0] // block):
        rows = slice(a * block, (a + 1) * block)
        part = low if a * block < half else high
        start = a * block % half
        out_ref[:, rows] = lax.dot_general(
            part[:, start : start + block], inverse_ref[rows, :], (((1,), (1,)), ((), ())), preferred_element_type=F32
        )


def solve_ancestor(mine, other, inverse):
    return pl.pallas_call(
        ancestor_kernel,
        out_shape=jax.ShapeDtypeStruct((mine.shape[0], inverse.shape[0]), F32),
        in_specs=[vmem_spec()] * 3,
        out_specs=vmem_spec(),
        compiler_params=pltpu.CompilerParams(vmem_limit_bytes=SMALL_LIMIT),
        name="ancestor",
    )(mine, other, inverse)


def exchange(value, axis, size, mask):
    return lax.ppermute(value, axis, [(i, i ^ mask) for i in range(size)])


def gather_plan(size):
    far, mirror = size // 2, size - 2
    wanted = [(mirror, 0), (1, 0), (2, 0), (3, 2), (mirror + 1, mirror), (far, mirror), (far + 1, 1)]
    plan, held = [], {0}
    for mask, parent in wanted:
        if 0 < mask < size and mask not in held and parent in held:
            plan.append((mask, parent))
            held.add(mask)
    while len(held) < size:
        for mask in range(1, size):
            parents = [mask ^ (1 << k) for k in range(size.bit_length() - 1) if mask ^ (1 << k) in held]
            if mask not in held and parents:
                plan.append((mask, parents[0]))
                held.add(mask)
    return plan


def gathered(value, size):
    held = {0: value}
    for mask, parent in gather_plan(size):
        held[mask] = exchange(held[parent], "proc", size, mask ^ parent)
    return [held[m] for m in range(size)]


def per_device(
    layers,
    procs,
    owner,
    rhs_blocks,
    chain_blocks,
    diag_inverse,
    factor_blocks,
    col_index,
    row_index,
    anc_rhs,
    anc_inverse,
):
    ticks = owner.shape[1]
    block = chain_blocks.shape[1]
    anc_rows = anc_inverse.shape[0]
    columns = anc_rhs.shape[1]
    half = anc_rows // 2
    proc, layer = lax.axis_index("proc"), lax.axis_index("layer")

    held = gathered(operators(diag_inverse, chain_blocks, rhs_blocks), procs)
    group = grouped(row_index[0] * ticks + col_index[0], factor_blocks, ticks, anc_rows // block)
    solved_t, send, keep = solve(owner, held, group)

    total = (keep + exchange(send, "layer", layers, 1).astype(F32)).astype(BF16)
    parts = lax.all_to_all(total, "proc", 0, 0, tiled=True)
    solved_t, parts = lax.optimization_barrier((solved_t, parts))
    total = jnp.sum(parts.reshape(procs, columns, half).astype(F32), axis=0)
    for k in range(1, layers.bit_length() - 1):
        total = total + exchange(total, "layer", layers, 1 << k)
    anc_t = lax.dynamic_slice_in_dim(anc_rhs, layer % 2 * half, half, 0).T
    mine = (anc_t - total).astype(BF16)
    ancestor = solve_ancestor(mine, exchange(mine, "layer", layers, 1), anc_inverse).T
    solved = lax.dynamic_slice_in_dim(solved_t, proc * columns, columns, 0).T
    return solved, ancestor


def solution(mesh):
    placed = (
        P("layer", None),
        P(("layer", "proc"), None),
        P(("layer", "proc"), None),
        P(("layer", "proc"), None),
        P(("layer", "proc"), None),
        P(("layer", "proc"), None),
        P(("layer", "proc"), None),
        P(None, "proc"),
        P(),
    )
    return jax.shard_map(
        functools.partial(per_device, mesh.shape["layer"], mesh.shape["proc"]),
        mesh=mesh,
        in_specs=placed,
        out_specs=(P("layer", "proc"), P(None, "proc")),
        check_vma=False,
    )
```

```python
import functools

import jax
import jax.numpy as jnp
from jax import lax
from jax.experimental import pallas as pl
from jax.experimental.pallas import tpu as pltpu
from jax.sharding import PartitionSpec as P

BF16 = jnp.bfloat16
F32 = jnp.float32
VMEM_LIMIT = 24 * 1024 * 1024
SMALL_LIMIT = 8 * 1024 * 1024
OPERATOR_LIMIT = 60 * 1024 * 1024
GROUP_LIMIT = 50 * 1024 * 1024


def vmem_spec():
    return pl.BlockSpec(memory_space=pltpu.VMEM)


def smem_spec():
    return pl.BlockSpec(memory_space=pltpu.SMEM)


def operator_kernel(diag_ref, chain_ref, rhs_ref, out_ref, diag, chain, rhs, arrived):
    copies = [
        pltpu.make_async_copy(source, target, arrived.at[i])
        for i, (source, target) in enumerate([(diag_ref, diag), (chain_ref, chain), (rhs_ref, rhs)])
    ]
    for copy in copies:
        copy.start()
    for copy in copies:
        copy.wait()
    block = chain.shape[1]
    out_ref[:block, :] = (-jnp.dot(diag[...], chain[...], preferred_element_type=F32)).T.astype(BF16)
    out_ref[block:, :] = jnp.dot(diag[...], rhs[...], preferred_element_type=F32).T.astype(BF16)


def operators(diag_inverse, chain_blocks, rhs_blocks):
    block = chain_blocks.shape[0]
    inputs = (diag_inverse, chain_blocks, rhs_blocks)
    return pl.pallas_call(
        operator_kernel,
        out_shape=jax.ShapeDtypeStruct((block + rhs_blocks.shape[1], block), BF16),
        in_specs=[pl.BlockSpec(memory_space=pl.ANY)] * 3,
        out_specs=vmem_spec(),
        scratch_shapes=[pltpu.VMEM(i.shape, BF16) for i in inputs] + [pltpu.SemaphoreType.DMA((3,))],
        compiler_params=pltpu.CompilerParams(vmem_limit_bytes=OPERATOR_LIMIT),
        name="operators",
    )(*inputs)


def group_kernel(ticks, anc_count, pair_ref, factor_ref, out_ref, total, held, arrived):
    block = total.shape[1]
    chunks = arrived.shape[0]
    per_chunk = held.shape[0] // (chunks * block)

    def fetch(i):
        rows = pl.ds(pl.multiple_of(i * per_chunk * block, block), per_chunk * block)
        return pltpu.make_async_copy(factor_ref.at[rows], held.at[rows], arrived.at[i])

    for i in range(chunks):
        fetch(i).start()
    total[...] = jnp.zeros_like(total)

    def add(i, carry):
        fetch(i).wait()
        for j in range(per_chunk):
            k = i * per_chunk + j
            total[pair_ref[k]] += held[pl.ds(pl.multiple_of(k * block, block), block), :].astype(F32)
        return carry

    lax.fori_loop(0, chunks, add, 0)
    for a in range(anc_count):
        for t in range(ticks):
            out_ref[t * block : (t + 1) * block, a * block : (a + 1) * block] = total[a * ticks + t].T.astype(BF16)


def grouped(pair, factor_blocks, ticks, anc_count):
    count = pair.shape[0]
    block = factor_blocks.shape[1]
    chunks = next(count // s for s in (8, 5, 4, 2, 1) if count % s == 0)
    return pl.pallas_call(
        functools.partial(group_kernel, ticks, anc_count),
        out_shape=jax.ShapeDtypeStruct((ticks * block, anc_count * block), BF16),
        in_specs=[smem_spec(), pl.BlockSpec(memory_space=pl.ANY)],
        out_specs=vmem_spec(),
        scratch_shapes=[
            pltpu.VMEM((anc_count * ticks, block, block), F32),
            pltpu.VMEM(factor_blocks.shape, BF16),
            pltpu.SemaphoreType.DMA((chunks,)),
        ],
        compiler_params=pltpu.CompilerParams(vmem_limit_bytes=GROUP_LIMIT),
        cost_estimate=pl.CostEstimate(flops=factor_blocks.size, bytes_accessed=2 * factor_blocks.size, transcendentals=0),
        name="grouped",
    )(pair, factor_blocks)


def solve_kernel(ticks, owner_ref, group_ref, *refs):
    operator_refs, (x_ref, send_ref, keep_ref, product, chosen) = refs[:-5], refs[-5:]
    proc, core = lax.axis_index("proc"), lax.axis_index("layer") % 2
    block = chosen.shape[2]
    half = send_ref.shape[1]
    for t in range(ticks):
        for j, ref in enumerate(operator_refs):

            @pl.when(owner_ref[0, t] ^ proc == j)
            def _(t=t, ref=ref):
                chosen[t] = ref[...]

    def update(t):
        part = jnp.dot(x_ref[:, t * block : (t + 1) * block], group_ref[t * block : (t + 1) * block, :], preferred_element_type=F32)
        product[...] = part if t == 0 else product[...] + part

    for t in range(ticks):
        if t == 0:
            x_ref[:, :block] = chosen[0, block:, :]
        else:
            previous = x_ref[:, (t - 1) * block : t * block]
            value = jnp.dot(previous, chosen[t, :block, :], preferred_element_type=F32)
            x_ref[:, t * block : (t + 1) * block] = (chosen[t, block:, :].astype(F32) + value).astype(BF16)
            update(t - 1)
    update(ticks - 1)
    mine = pl.multiple_of(core * half, half)
    other = pl.multiple_of((1 - core) * half, half)
    keep_ref[...] = product[:, pl.ds(mine, half)]
    send_ref[...] = product[:, pl.ds(other, half)].astype(BF16)


def solve(owner, held, group):
    ticks = owner.shape[1]
    block = held[0].shape[1]
    rhs_width = held[0].shape[0] - block
    anc_rows = group.shape[1]
    return pl.pallas_call(
        functools.partial(solve_kernel, ticks),
        out_shape=(
            jax.ShapeDtypeStruct((rhs_width, ticks * block), BF16),
            jax.ShapeDtypeStruct((rhs_width, anc_rows // 2), BF16),
            jax.ShapeDtypeStruct((rhs_width, anc_rows // 2), F32),
        ),
        in_specs=[smem_spec()] + [vmem_spec()] * (1 + len(held)),
        out_specs=(vmem_spec(), vmem_spec(), vmem_spec()),
        scratch_shapes=[
            pltpu.VMEM((rhs_width, anc_rows), F32),
            pltpu.VMEM((ticks, *held[0].shape), BF16),
        ],
        compiler_params=pltpu.CompilerParams(vmem_limit_bytes=VMEM_LIMIT),
        name="solve",
    )(owner, group, *held)


def ancestor_kernel(mine_ref, other_ref, inverse_ref, out_ref):
    block = inverse_ref.shape[1]
    half = mine_ref.shape[1]
    first = lax.axis_index("layer") % 2 == 0
    mine, other = mine_ref[...], other_ref[...]
    low, high = jnp.where(first, mine, other), jnp.where(first, other, mine)
    for a in range(inverse_ref.shape[0] // block):
        rows = slice(a * block, (a + 1) * block)
        part = low if a * block < half else high
        start = a * block % half
        out_ref[:, rows] = lax.dot_general(
            part[:, start : start + block], inverse_ref[rows, :], (((1,), (1,)), ((), ())), preferred_element_type=F32
        )


def solve_ancestor(mine, other, inverse):
    return pl.pallas_call(
        ancestor_kernel,
        out_shape=jax.ShapeDtypeStruct((mine.shape[0], inverse.shape[0]), F32),
        in_specs=[vmem_spec()] * 3,
        out_specs=vmem_spec(),
        compiler_params=pltpu.CompilerParams(vmem_limit_bytes=SMALL_LIMIT),
        name="ancestor",
    )(mine, other, inverse)


def exchange(value, axis, size, mask):
    return lax.ppermute(value, axis, [(i, i ^ mask) for i in range(size)])


def gather_plan(size):
    far, mirror = size // 2, size - 2
    wanted = [(mirror, 0), (1, 0), (2, 0), (far + 1, 1), (3, 2), (mirror + 1, mirror), (far, mirror)]
    plan, held = [], {0}
    for mask, parent in wanted:
        if 0 < mask < size and mask not in held and parent in held:
            plan.append((mask, parent))
            held.add(mask)
    while len(held) < size:
        for mask in range(1, size):
            parents = [mask ^ (1 << k) for k in range(size.bit_length() - 1) if mask ^ (1 << k) in held]
            if mask not in held and parents:
                plan.append((mask, parents[0]))
                held.add(mask)
    return plan


def gathered(value, size, make_group):
    held, group = {0: value}, None
    for mask, parent in gather_plan(size):
        if parent and group is None:
            group, held[1] = lax.optimization_barrier((make_group(), held[1]))
        held[mask] = exchange(held[parent], "proc", size, mask ^ parent)
    return [held[m] for m in range(size)], make_group() if group is None else group


def per_device(
    layers,
    procs,
    owner,
    rhs_blocks,
    chain_blocks,
    diag_inverse,
    factor_blocks,
    col_index,
    row_index,
    anc_rhs,
    anc_inverse,
):
    ticks = owner.shape[1]
    block = chain_blocks.shape[1]
    anc_rows = anc_inverse.shape[0]
    columns = anc_rhs.shape[1]
    half = anc_rows // 2
    proc, layer = lax.axis_index("proc"), lax.axis_index("layer")

    held, group = gathered(
        operators(diag_inverse, chain_blocks, rhs_blocks),
        procs,
        lambda: grouped(row_index[0] * ticks + col_index[0], factor_blocks, ticks, anc_rows // block),
    )
    solved_t, send, keep = solve(owner, held, group)

    total = (keep + exchange(send, "layer", layers, 1).astype(F32)).astype(BF16)
    parts = lax.all_to_all(total, "proc", 0, 0, tiled=True)
    solved_t, parts = lax.optimization_barrier((solved_t, parts))
    total = jnp.sum(parts.reshape(procs, columns, half).astype(F32), axis=0)
    for k in range(1, layers.bit_length() - 1):
        total = total + exchange(total, "layer", layers, 1 << k)
    anc_t = lax.dynamic_slice_in_dim(anc_rhs, layer % 2 * half, half, 0).T
    mine = (anc_t - total).astype(BF16)
    ancestor = solve_ancestor(mine, exchange(mine, "layer", layers, 1), anc_inverse).T
    solved = lax.dynamic_slice_in_dim(solved_t, proc * columns, columns, 0).T
    return solved, ancestor


def solution(mesh):
    placed = (
        P("layer", None),
        P(("layer", "proc"), None),
        P(("layer", "proc"), None),
        P(("layer", "proc"), None),
        P(("layer", "proc"), None),
        P(("layer", "proc"), None),
        P(("layer", "proc"), None),
        P(None, "proc"),
        P(),
    )
    return jax.shard_map(
        functools.partial(per_device, mesh.shape["layer"], mesh.shape["proc"]),
        mesh=mesh,
        in_specs=placed,
        out_specs=(P("layer", "proc"), P(None, "proc")),
        check_vma=False,
    )
```

```python
import functools

import jax
import jax.numpy as jnp
from jax import lax
from jax.experimental import pallas as pl
from jax.experimental.pallas import tpu as pltpu
from jax.sharding import PartitionSpec as P

BF16 = jnp.bfloat16
F32 = jnp.float32
VMEM_LIMIT = 24 * 1024 * 1024
SMALL_LIMIT = 8 * 1024 * 1024
GROUP_LIMIT = 50 * 1024 * 1024


def vmem_spec():
    return pl.BlockSpec(memory_space=pltpu.VMEM)


def smem_spec():
    return pl.BlockSpec(memory_space=pltpu.SMEM)


def operator_kernel(diag_ref, chain_ref, rhs_ref, out_ref, diag, chain, rhs, arrived):
    copies = [
        pltpu.make_async_copy(source, target, arrived.at[i])
        for i, (source, target) in enumerate([(diag_ref, diag), (chain_ref, chain), (rhs_ref, rhs)])
    ]
    for copy in copies:
        copy.start()
    for copy in copies:
        copy.wait()
    block = chain.shape[1]
    out_ref[:block, :] = (-jnp.dot(diag[...], chain[...], preferred_element_type=F32)).T.astype(BF16)
    out_ref[block:, :] = jnp.dot(diag[...], rhs[...], preferred_element_type=F32).T.astype(BF16)


def operators(diag_inverse, chain_blocks, rhs_blocks):
    block = chain_blocks.shape[0]
    inputs = [pltpu.with_memory_space_constraint(i, pltpu.HBM) for i in (diag_inverse, chain_blocks, rhs_blocks)]
    return pl.pallas_call(
        operator_kernel,
        out_shape=jax.ShapeDtypeStruct((block + rhs_blocks.shape[1], block), BF16),
        in_specs=[pl.BlockSpec(memory_space=pl.ANY)] * 3,
        out_specs=vmem_spec(),
        scratch_shapes=[pltpu.VMEM(i.shape, BF16) for i in inputs] + [pltpu.SemaphoreType.DMA((3,))],
        compiler_params=pltpu.CompilerParams(vmem_limit_bytes=SMALL_LIMIT),
        name="operators",
    )(*inputs)


def group_kernel(ticks, anc_count, pair_ref, factor_ref, out_ref, total, held, arrived):
    block = total.shape[1]
    chunks = arrived.shape[0]
    per_chunk = held.shape[0] // (chunks * block)

    def fetch(i):
        rows = pl.ds(pl.multiple_of(i * per_chunk * block, block), per_chunk * block)
        return pltpu.make_async_copy(factor_ref.at[rows], held.at[rows], arrived.at[i])

    for i in range(chunks):
        fetch(i).start()
    total[...] = jnp.zeros_like(total)

    def add(i, carry):
        fetch(i).wait()
        for j in range(per_chunk):
            k = i * per_chunk + j
            total[pair_ref[k]] += held[pl.ds(pl.multiple_of(k * block, block), block), :].astype(F32)
        return carry

    lax.fori_loop(0, chunks, add, 0)
    for a in range(anc_count):
        for t in range(ticks):
            out_ref[t * block : (t + 1) * block, a * block : (a + 1) * block] = total[a * ticks + t].T.astype(BF16)


def grouped(pair, factor_blocks, ticks, anc_count):
    count = pair.shape[0]
    block = factor_blocks.shape[1]
    chunks = next(count // s for s in (8, 5, 4, 2, 1) if count % s == 0)
    return pl.pallas_call(
        functools.partial(group_kernel, ticks, anc_count),
        out_shape=jax.ShapeDtypeStruct((ticks * block, anc_count * block), BF16),
        in_specs=[smem_spec(), pl.BlockSpec(memory_space=pl.ANY)],
        out_specs=vmem_spec(),
        scratch_shapes=[
            pltpu.VMEM((anc_count * ticks, block, block), F32),
            pltpu.VMEM(factor_blocks.shape, BF16),
            pltpu.SemaphoreType.DMA((chunks,)),
        ],
        compiler_params=pltpu.CompilerParams(vmem_limit_bytes=GROUP_LIMIT),
        cost_estimate=pl.CostEstimate(flops=factor_blocks.size, bytes_accessed=2 * factor_blocks.size, transcendentals=0),
        name="grouped",
    )(pair, factor_blocks)


def solve_kernel(ticks, owner_ref, group_ref, *refs):
    operator_refs, (x_ref, send_ref, keep_ref, product, chosen) = refs[:-5], refs[-5:]
    proc, core = lax.axis_index("proc"), lax.axis_index("layer") % 2
    block = chosen.shape[2]
    half = send_ref.shape[1]
    for t in range(ticks):
        for j, ref in enumerate(operator_refs):

            @pl.when(owner_ref[0, t] ^ proc == j)
            def _(t=t, ref=ref):
                chosen[t] = ref[...]

    def update(t):
        part = jnp.dot(x_ref[:, t * block : (t + 1) * block], group_ref[t * block : (t + 1) * block, :], preferred_element_type=F32)
        product[...] = part if t == 0 else product[...] + part

    for t in range(ticks):
        if t == 0:
            x_ref[:, :block] = chosen[0, block:, :]
        else:
            previous = x_ref[:, (t - 1) * block : t * block]
            value = jnp.dot(previous, chosen[t, :block, :], preferred_element_type=F32)
            x_ref[:, t * block : (t + 1) * block] = (chosen[t, block:, :].astype(F32) + value).astype(BF16)
            update(t - 1)
    update(ticks - 1)
    mine = pl.multiple_of(core * half, half)
    other = pl.multiple_of((1 - core) * half, half)
    keep_ref[...] = product[:, pl.ds(mine, half)]
    send_ref[...] = product[:, pl.ds(other, half)].astype(BF16)


def solve(owner, held, group):
    ticks = owner.shape[1]
    block = held[0].shape[1]
    rhs_width = held[0].shape[0] - block
    anc_rows = group.shape[1]
    return pl.pallas_call(
        functools.partial(solve_kernel, ticks),
        out_shape=(
            jax.ShapeDtypeStruct((rhs_width, ticks * block), BF16),
            jax.ShapeDtypeStruct((rhs_width, anc_rows // 2), BF16),
            jax.ShapeDtypeStruct((rhs_width, anc_rows // 2), F32),
        ),
        in_specs=[smem_spec()] + [vmem_spec()] * (1 + len(held)),
        out_specs=(vmem_spec(), vmem_spec(), vmem_spec()),
        scratch_shapes=[
            pltpu.VMEM((rhs_width, anc_rows), F32),
            pltpu.VMEM((ticks, *held[0].shape), BF16),
        ],
        compiler_params=pltpu.CompilerParams(vmem_limit_bytes=VMEM_LIMIT),
        name="solve",
    )(owner, group, *held)


def ancestor_kernel(mine_ref, other_ref, inverse_ref, out_ref):
    block = inverse_ref.shape[1]
    half = mine_ref.shape[1]
    first = lax.axis_index("layer") % 2 == 0
    mine, other = mine_ref[...], other_ref[...]
    low, high = jnp.where(first, mine, other), jnp.where(first, other, mine)
    for a in range(inverse_ref.shape[0] // block):
        rows = slice(a * block, (a + 1) * block)
        part = low if a * block < half else high
        start = a * block % half
        out_ref[:, rows] = lax.dot_general(
            part[:, start : start + block], inverse_ref[rows, :], (((1,), (1,)), ((), ())), preferred_element_type=F32
        )


def solve_ancestor(mine, other, inverse):
    return pl.pallas_call(
        ancestor_kernel,
        out_shape=jax.ShapeDtypeStruct((mine.shape[0], inverse.shape[0]), F32),
        in_specs=[vmem_spec()] * 3,
        out_specs=vmem_spec(),
        compiler_params=pltpu.CompilerParams(vmem_limit_bytes=SMALL_LIMIT),
        name="ancestor",
    )(mine, other, inverse)


def exchange(value, axis, size, mask):
    return lax.ppermute(value, axis, [(i, i ^ mask) for i in range(size)])


def gather_plan(size):
    far, mirror = size // 2, size - 2
    wanted = [(mirror, 0), (1, 0), (2, 0), (far + 1, 1), (3, 2), (mirror + 1, mirror), (far, mirror)]
    plan, held = [], {0}
    for mask, parent in wanted:
        if 0 < mask < size and mask not in held and parent in held:
            plan.append((mask, parent))
            held.add(mask)
    while len(held) < size:
        for mask in range(1, size):
            parents = [mask ^ (1 << k) for k in range(size.bit_length() - 1) if mask ^ (1 << k) in held]
            if mask not in held and parents:
                plan.append((mask, parents[0]))
                held.add(mask)
    return plan


def gathered(value, size, make_group):
    held, group = {0: value}, None
    for mask, parent in gather_plan(size):
        if parent and group is None:
            group, held[1] = lax.optimization_barrier((make_group(), held[1]))
        held[mask] = exchange(held[parent], "proc", size, mask ^ parent)
    return [held[m] for m in range(size)], make_group() if group is None else group


def per_device(
    layers,
    procs,
    owner,
    rhs_blocks,
    chain_blocks,
    diag_inverse,
    factor_blocks,
    col_index,
    row_index,
    anc_rhs,
    anc_inverse,
):
    ticks = owner.shape[1]
    block = chain_blocks.shape[1]
    anc_rows = anc_inverse.shape[0]
    columns = anc_rhs.shape[1]
    half = anc_rows // 2
    proc, layer = lax.axis_index("proc"), lax.axis_index("layer")

    held, group = gathered(
        operators(diag_inverse, chain_blocks, rhs_blocks),
        procs,
        lambda: grouped(row_index[0] * ticks + col_index[0], factor_blocks, ticks, anc_rows // block),
    )
    solved_t, send, keep = solve(owner, held, group)

    total = (keep + exchange(send, "layer", layers, 1).astype(F32)).astype(BF16)
    parts = lax.all_to_all(total, "proc", 0, 0, tiled=True)
    solved_t, parts = lax.optimization_barrier((solved_t, parts))
    total = jnp.sum(parts.reshape(procs, columns, half).astype(F32), axis=0)
    for k in range(1, layers.bit_length() - 1):
        total = total + exchange(total, "layer", layers, 1 << k)
    anc_t = lax.dynamic_slice_in_dim(anc_rhs, layer % 2 * half, half, 0).T
    mine = (anc_t - total).astype(BF16)
    ancestor = solve_ancestor(mine, exchange(mine, "layer", layers, 1), anc_inverse).T
    solved = lax.dynamic_slice_in_dim(solved_t, proc * columns, columns, 0).T
    return solved, ancestor


def solution(mesh):
    placed = (
        P("layer", None),
        P(("layer", "proc"), None),
        P(("layer", "proc"), None),
        P(("layer", "proc"), None),
        P(("layer", "proc"), None),
        P(("layer", "proc"), None),
        P(("layer", "proc"), None),
        P(None, "proc"),
        P(),
    )
    return jax.shard_map(
        functools.partial(per_device, mesh.shape["layer"], mesh.shape["proc"]),
        mesh=mesh,
        in_specs=placed,
        out_specs=(P("layer", "proc"), P(None, "proc")),
        check_vma=False,
    )
```

```python
import functools

import jax
import jax.numpy as jnp
from jax import lax
from jax.experimental import pallas as pl
from jax.experimental.pallas import tpu as pltpu
from jax.sharding import PartitionSpec as P

BF16 = jnp.bfloat16
F32 = jnp.float32
VMEM_LIMIT = 24 * 1024 * 1024
SMALL_LIMIT = 8 * 1024 * 1024
GROUP_LIMIT = 50 * 1024 * 1024


def vmem_spec():
    return pl.BlockSpec(memory_space=pltpu.VMEM)


def smem_spec():
    return pl.BlockSpec(memory_space=pltpu.SMEM)


def operator_kernel(diag_ref, chain_ref, rhs_ref, out_ref, diag, chain, rhs, arrived):
    copies = [
        pltpu.make_async_copy(source, target, arrived.at[i])
        for i, (source, target) in enumerate([(diag_ref, diag), (chain_ref, chain), (rhs_ref, rhs)])
    ]
    for copy in copies:
        copy.start()
    for copy in copies:
        copy.wait()
    block = chain.shape[1]
    out_ref[:block, :] = (-jnp.dot(diag[...], chain[...], preferred_element_type=F32)).T.astype(BF16)
    out_ref[block:, :] = jnp.dot(diag[...], rhs[...], preferred_element_type=F32).T.astype(BF16)


def operators(diag_inverse, chain_blocks, rhs_blocks):
    block = chain_blocks.shape[0]
    inputs = [pltpu.with_memory_space_constraint(i, pltpu.HBM) for i in (diag_inverse, chain_blocks, rhs_blocks)]
    return pl.pallas_call(
        operator_kernel,
        out_shape=jax.ShapeDtypeStruct((block + rhs_blocks.shape[1], block), BF16),
        in_specs=[pl.BlockSpec(memory_space=pl.ANY)] * 3,
        out_specs=vmem_spec(),
        scratch_shapes=[pltpu.VMEM(i.shape, BF16) for i in inputs] + [pltpu.SemaphoreType.DMA((3,))],
        compiler_params=pltpu.CompilerParams(vmem_limit_bytes=SMALL_LIMIT),
        name="operators",
    )(*inputs)


def group_kernel(ticks, anc_count, pair_ref, factor_ref, out_ref, total, held, arrived):
    block = total.shape[1]
    chunks = arrived.shape[0]
    per_chunk = held.shape[0] // (chunks * block)

    def fetch(i):
        rows = pl.ds(pl.multiple_of(i * per_chunk * block, block), per_chunk * block)
        return pltpu.make_async_copy(factor_ref.at[rows], held.at[rows], arrived.at[i])

    for i in range(chunks):
        fetch(i).start()
    total[...] = jnp.zeros_like(total)

    def add(i, carry):
        fetch(i).wait()
        for j in range(per_chunk):
            k = i * per_chunk + j
            total[pair_ref[k]] += held[pl.ds(pl.multiple_of(k * block, block), block), :].astype(F32)
        return carry

    lax.fori_loop(0, chunks, add, 0)
    for a in range(anc_count):
        for t in range(ticks):
            out_ref[t * block : (t + 1) * block, a * block : (a + 1) * block] = total[a * ticks + t].T.astype(BF16)


def grouped(pair, factor_blocks, ticks, anc_count):
    count = pair.shape[0]
    block = factor_blocks.shape[1]
    chunks = next(count // s for s in (8, 5, 4, 2, 1) if count % s == 0)
    return pl.pallas_call(
        functools.partial(group_kernel, ticks, anc_count),
        out_shape=jax.ShapeDtypeStruct((ticks * block, anc_count * block), BF16),
        in_specs=[smem_spec(), pl.BlockSpec(memory_space=pl.ANY)],
        out_specs=vmem_spec(),
        scratch_shapes=[
            pltpu.VMEM((anc_count * ticks, block, block), F32),
            pltpu.VMEM(factor_blocks.shape, BF16),
            pltpu.SemaphoreType.DMA((chunks,)),
        ],
        compiler_params=pltpu.CompilerParams(vmem_limit_bytes=GROUP_LIMIT),
        cost_estimate=pl.CostEstimate(flops=factor_blocks.size, bytes_accessed=2 * factor_blocks.size, transcendentals=0),
        name="grouped",
    )(pair, factor_blocks)


def solve_kernel(ticks, owner_ref, group_ref, *refs):
    operator_refs, (x_ref, send_ref, keep_ref, product, chosen) = refs[:-5], refs[-5:]
    proc, core = lax.axis_index("proc"), lax.axis_index("layer") % 2
    block = chosen.shape[2]
    half = send_ref.shape[1]
    for t in range(ticks):
        for j, ref in enumerate(operator_refs):

            @pl.when(owner_ref[0, t] ^ proc == j)
            def _(t=t, ref=ref):
                chosen[t] = ref[...]

    def update(t):
        part = jnp.dot(x_ref[:, t * block : (t + 1) * block], group_ref[t * block : (t + 1) * block, :], preferred_element_type=F32)
        product[...] = part if t == 0 else product[...] + part

    for t in range(ticks):
        if t == 0:
            x_ref[:, :block] = chosen[0, block:, :]
        else:
            previous = x_ref[:, (t - 1) * block : t * block]
            value = jnp.dot(previous, chosen[t, :block, :], preferred_element_type=F32)
            x_ref[:, t * block : (t + 1) * block] = (chosen[t, block:, :].astype(F32) + value).astype(BF16)
            update(t - 1)
    update(ticks - 1)
    mine = pl.multiple_of(core * half, half)
    other = pl.multiple_of((1 - core) * half, half)
    keep_ref[...] = product[:, pl.ds(mine, half)]
    send_ref[...] = product[:, pl.ds(other, half)].astype(BF16)


def solve(owner, held, group):
    ticks = owner.shape[1]
    block = held[0].shape[1]
    rhs_width = held[0].shape[0] - block
    anc_rows = group.shape[1]
    return pl.pallas_call(
        functools.partial(solve_kernel, ticks),
        out_shape=(
            jax.ShapeDtypeStruct((rhs_width, ticks * block), BF16),
            jax.ShapeDtypeStruct((rhs_width, anc_rows // 2), BF16),
            jax.ShapeDtypeStruct((rhs_width, anc_rows // 2), F32),
        ),
        in_specs=[smem_spec()] + [vmem_spec()] * (1 + len(held)),
        out_specs=(vmem_spec(), vmem_spec(), vmem_spec()),
        scratch_shapes=[
            pltpu.VMEM((rhs_width, anc_rows), F32),
            pltpu.VMEM((ticks, *held[0].shape), BF16),
        ],
        compiler_params=pltpu.CompilerParams(vmem_limit_bytes=VMEM_LIMIT),
        name="solve",
    )(owner, group, *held)


def ancestor_kernel(mine_ref, other_ref, inverse_ref, out_ref):
    block = inverse_ref.shape[1]
    half = mine_ref.shape[1]
    first = lax.axis_index("layer") % 2 == 0
    mine, other = mine_ref[...], other_ref[...]
    low, high = jnp.where(first, mine, other), jnp.where(first, other, mine)
    for a in range(inverse_ref.shape[0] // block):
        rows = slice(a * block, (a + 1) * block)
        part = low if a * block < half else high
        start = a * block % half
        out_ref[:, rows] = lax.dot_general(
            part[:, start : start + block], inverse_ref[rows, :], (((1,), (1,)), ((), ())), preferred_element_type=F32
        )


def solve_ancestor(mine, other, inverse):
    return pl.pallas_call(
        ancestor_kernel,
        out_shape=jax.ShapeDtypeStruct((mine.shape[0], inverse.shape[0]), F32),
        in_specs=[vmem_spec()] * 3,
        out_specs=vmem_spec(),
        compiler_params=pltpu.CompilerParams(vmem_limit_bytes=SMALL_LIMIT),
        name="ancestor",
    )(mine, other, inverse)


def exchange(value, axis, size, mask):
    return lax.ppermute(value, axis, [(i, i ^ mask) for i in range(size)])


def gather_plan(size):
    far, mirror = size // 2, size - 2
    wanted = [(mirror, 0), (1, 0), (2, 0), (far + 1, 1), (3, 2), (mirror + 1, mirror), (far, mirror)]
    plan, held = [], {0}
    for mask, parent in wanted:
        if 0 < mask < size and mask not in held and parent in held:
            plan.append((mask, parent))
            held.add(mask)
    while len(held) < size:
        for mask in range(1, size):
            parents = [mask ^ (1 << k) for k in range(size.bit_length() - 1) if mask ^ (1 << k) in held]
            if mask not in held and parents:
                plan.append((mask, parents[0]))
                held.add(mask)
    return plan


def gathered(value, size, make_group):
    held, group = {0: value}, None
    for mask, parent in gather_plan(size):
        if parent and group is None:
            group, held[1] = lax.optimization_barrier((make_group(), held[1]))
        held[mask] = exchange(held[parent], "proc", size, mask ^ parent)
    return [held[m] for m in range(size)], make_group() if group is None else group


def per_device(
    layers,
    procs,
    owner,
    rhs_blocks,
    chain_blocks,
    diag_inverse,
    factor_blocks,
    col_index,
    row_index,
    anc_rhs,
    anc_inverse,
):
    ticks = owner.shape[1]
    block = chain_blocks.shape[1]
    anc_rows = anc_inverse.shape[0]
    columns = anc_rhs.shape[1]
    half = anc_rows // 2
    proc, layer = lax.axis_index("proc"), lax.axis_index("layer")

    held, group = gathered(
        operators(diag_inverse, chain_blocks, rhs_blocks),
        procs,
        lambda: grouped(row_index[0] * ticks + col_index[0], factor_blocks, ticks, anc_rows // block),
    )
    solved_t, send, keep = solve(owner, held, group)

    total = (keep + exchange(send, "layer", layers, 1).astype(F32)).astype(BF16)
    parts = lax.all_to_all(total, "proc", 0, 0, tiled=True)
    solved_t, parts = lax.optimization_barrier((solved_t, parts))
    total = jnp.sum(parts.reshape(procs, columns, half).astype(F32), axis=0)
    for k in range(1, layers.bit_length() - 1):
        total = total.astype(BF16)
        total = total.astype(F32) + exchange(total, "layer", layers, 1 << k).astype(F32)
    anc_t = lax.dynamic_slice_in_dim(anc_rhs, layer % 2 * half, half, 0).T
    mine = (anc_t - total).astype(BF16)
    ancestor = solve_ancestor(mine, exchange(mine, "layer", layers, 1), anc_inverse).T
    solved = lax.dynamic_slice_in_dim(solved_t, proc * columns, columns, 0).T
    return solved, ancestor


def solution(mesh):
    placed = (
        P("layer", None),
        P(("layer", "proc"), None),
        P(("layer", "proc"), None),
        P(("layer", "proc"), None),
        P(("layer", "proc"), None),
        P(("layer", "proc"), None),
        P(("layer", "proc"), None),
        P(None, "proc"),
        P(),
    )
    return jax.shard_map(
        functools.partial(per_device, mesh.shape["layer"], mesh.shape["proc"]),
        mesh=mesh,
        in_specs=placed,
        out_specs=(P("layer", "proc"), P(None, "proc")),
        check_vma=False,
    )
```

```python
import functools

import jax
import jax.numpy as jnp
from jax import lax
from jax.experimental import pallas as pl
from jax.experimental.pallas import tpu as pltpu
from jax.sharding import PartitionSpec as P

BF16 = jnp.bfloat16
F32 = jnp.float32
VMEM_LIMIT = 24 * 1024 * 1024
SMALL_LIMIT = 8 * 1024 * 1024
GROUP_LIMIT = 50 * 1024 * 1024


def vmem_spec():
    return pl.BlockSpec(memory_space=pltpu.VMEM)


def smem_spec():
    return pl.BlockSpec(memory_space=pltpu.SMEM)


def operator_kernel(diag_ref, chain_ref, rhs_ref, out_ref, diag, chain, rhs, arrived):
    copies = [
        pltpu.make_async_copy(source, target, arrived.at[i])
        for i, (source, target) in enumerate([(diag_ref, diag), (chain_ref, chain), (rhs_ref, rhs)])
    ]
    for copy in copies:
        copy.start()
    for copy in copies:
        copy.wait()
    block = chain.shape[1]
    out_ref[:block, :] = (-jnp.dot(diag[...], chain[...], preferred_element_type=F32)).T.astype(BF16)
    out_ref[block:, :] = jnp.dot(diag[...], rhs[...], preferred_element_type=F32).T.astype(BF16)


def operators(diag_inverse, chain_blocks, rhs_blocks):
    block = chain_blocks.shape[0]
    inputs = [pltpu.with_memory_space_constraint(i, pltpu.HBM) for i in (diag_inverse, chain_blocks, rhs_blocks)]
    return pl.pallas_call(
        operator_kernel,
        out_shape=jax.ShapeDtypeStruct((block + rhs_blocks.shape[1], block), BF16),
        in_specs=[pl.BlockSpec(memory_space=pl.ANY)] * 3,
        out_specs=vmem_spec(),
        scratch_shapes=[pltpu.VMEM(i.shape, BF16) for i in inputs] + [pltpu.SemaphoreType.DMA((3,))],
        compiler_params=pltpu.CompilerParams(vmem_limit_bytes=SMALL_LIMIT),
        name="operators",
    )(*inputs)


def group_kernel(ticks, anc_count, pair_ref, factor_ref, out_ref, total, held, arrived):
    block = total.shape[1]
    chunks = arrived.shape[0]
    per_chunk = held.shape[0] // (chunks * block)

    def fetch(i):
        rows = pl.ds(pl.multiple_of(i * per_chunk * block, block), per_chunk * block)
        return pltpu.make_async_copy(factor_ref.at[rows], held.at[rows], arrived.at[i])

    for i in range(chunks):
        fetch(i).start()
    total[...] = jnp.zeros_like(total)

    def add(i, carry):
        fetch(i).wait()
        for j in range(per_chunk):
            k = i * per_chunk + j
            total[pair_ref[k]] += held[pl.ds(pl.multiple_of(k * block, block), block), :].astype(F32)
        return carry

    lax.fori_loop(0, chunks, add, 0)
    for a in range(anc_count):
        for t in range(ticks):
            out_ref[t * block : (t + 1) * block, a * block : (a + 1) * block] = total[a * ticks + t].T.astype(BF16)


def grouped(pair, factor_blocks, ticks, anc_count):
    count = pair.shape[0]
    block = factor_blocks.shape[1]
    chunks = next(count // s for s in (8, 5, 4, 2, 1) if count % s == 0)
    return pl.pallas_call(
        functools.partial(group_kernel, ticks, anc_count),
        out_shape=jax.ShapeDtypeStruct((ticks * block, anc_count * block), BF16),
        in_specs=[smem_spec(), pl.BlockSpec(memory_space=pl.ANY)],
        out_specs=vmem_spec(),
        scratch_shapes=[
            pltpu.VMEM((anc_count * ticks, block, block), F32),
            pltpu.VMEM(factor_blocks.shape, BF16),
            pltpu.SemaphoreType.DMA((chunks,)),
        ],
        compiler_params=pltpu.CompilerParams(vmem_limit_bytes=GROUP_LIMIT),
        cost_estimate=pl.CostEstimate(flops=factor_blocks.size, bytes_accessed=2 * factor_blocks.size, transcendentals=0),
        name="grouped",
    )(pair, factor_blocks)


def solve_kernel(ticks, owner_ref, group_ref, *refs):
    operator_refs, (x_ref, send_ref, keep_ref, product, chosen) = refs[:-5], refs[-5:]
    proc, core = lax.axis_index("proc"), lax.axis_index("layer") % 2
    block = chosen.shape[2]
    half = send_ref.shape[1]
    for t in range(ticks):
        for j, ref in enumerate(operator_refs):

            @pl.when(owner_ref[0, t] ^ proc == j)
            def _(t=t, ref=ref):
                chosen[t] = ref[...]

    def update(t):
        part = jnp.dot(x_ref[:, t * block : (t + 1) * block], group_ref[t * block : (t + 1) * block, :], preferred_element_type=F32)
        product[...] = part if t == 0 else product[...] + part

    for t in range(ticks):
        if t == 0:
            x_ref[:, :block] = chosen[0, block:, :]
        else:
            previous = x_ref[:, (t - 1) * block : t * block]
            value = jnp.dot(previous, chosen[t, :block, :], preferred_element_type=F32)
            x_ref[:, t * block : (t + 1) * block] = (chosen[t, block:, :].astype(F32) + value).astype(BF16)
            update(t - 1)
    update(ticks - 1)
    mine = pl.multiple_of(core * half, half)
    other = pl.multiple_of((1 - core) * half, half)
    keep_ref[...] = product[:, pl.ds(mine, half)]
    send_ref[...] = product[:, pl.ds(other, half)].astype(BF16)


def solve(owner, held, group):
    ticks = owner.shape[1]
    block = held[0].shape[1]
    rhs_width = held[0].shape[0] - block
    anc_rows = group.shape[1]
    return pl.pallas_call(
        functools.partial(solve_kernel, ticks),
        out_shape=(
            jax.ShapeDtypeStruct((rhs_width, ticks * block), BF16),
            jax.ShapeDtypeStruct((rhs_width, anc_rows // 2), BF16),
            jax.ShapeDtypeStruct((rhs_width, anc_rows // 2), F32),
        ),
        in_specs=[smem_spec()] + [vmem_spec()] * (1 + len(held)),
        out_specs=(vmem_spec(), vmem_spec(), vmem_spec()),
        scratch_shapes=[
            pltpu.VMEM((rhs_width, anc_rows), F32),
            pltpu.VMEM((ticks, *held[0].shape), BF16),
        ],
        compiler_params=pltpu.CompilerParams(vmem_limit_bytes=VMEM_LIMIT),
        name="solve",
    )(owner, group, *held)


def ancestor_kernel(mine_ref, other_ref, inverse_ref, out_ref):
    block = inverse_ref.shape[1]
    half = mine_ref.shape[1]
    first = lax.axis_index("layer") % 2 == 0
    mine, other = mine_ref[...], other_ref[...]
    low, high = jnp.where(first, mine, other), jnp.where(first, other, mine)
    for a in range(inverse_ref.shape[0] // block):
        rows = slice(a * block, (a + 1) * block)
        part = low if a * block < half else high
        start = a * block % half
        out_ref[:, rows] = lax.dot_general(
            part[:, start : start + block], inverse_ref[rows, :], (((1,), (1,)), ((), ())), preferred_element_type=F32
        )


def solve_ancestor(mine, other, inverse):
    return pl.pallas_call(
        ancestor_kernel,
        out_shape=jax.ShapeDtypeStruct((mine.shape[0], inverse.shape[0]), F32),
        in_specs=[vmem_spec()] * 3,
        out_specs=vmem_spec(),
        compiler_params=pltpu.CompilerParams(vmem_limit_bytes=SMALL_LIMIT),
        name="ancestor",
    )(mine, other, inverse)


def exchange(value, axis, size, mask):
    return lax.ppermute(value, axis, [(i, i ^ mask) for i in range(size)])


def gather_plan(size):
    far, mirror = size // 2, size - 2
    wanted = [(mirror, 0), (1, 0), (2, 0), (far + 1, 1), (far, mirror), (mirror + 1, mirror), (3, 2)]
    plan, held = [], {0}
    for mask, parent in wanted:
        if 0 < mask < size and mask not in held and parent in held:
            plan.append((mask, parent))
            held.add(mask)
    while len(held) < size:
        for mask in range(1, size):
            parents = [mask ^ (1 << k) for k in range(size.bit_length() - 1) if mask ^ (1 << k) in held]
            if mask not in held and parents:
                plan.append((mask, parents[0]))
                held.add(mask)
    return plan


def gathered(value, size, make_group):
    held, group = {0: value}, None
    for mask, parent in gather_plan(size):
        if parent and group is None:
            group, held[1] = lax.optimization_barrier((make_group(), held[1]))
        held[mask] = exchange(held[parent], "proc", size, mask ^ parent)
    return [held[m] for m in range(size)], make_group() if group is None else group


def per_device(
    layers,
    procs,
    owner,
    rhs_blocks,
    chain_blocks,
    diag_inverse,
    factor_blocks,
    col_index,
    row_index,
    anc_rhs,
    anc_inverse,
):
    ticks = owner.shape[1]
    block = chain_blocks.shape[1]
    anc_rows = anc_inverse.shape[0]
    columns = anc_rhs.shape[1]
    half = anc_rows // 2
    proc, layer = lax.axis_index("proc"), lax.axis_index("layer")

    held, group = gathered(
        operators(diag_inverse, chain_blocks, rhs_blocks),
        procs,
        lambda: grouped(row_index[0] * ticks + col_index[0], factor_blocks, ticks, anc_rows // block),
    )
    solved_t, send, keep = solve(owner, held, group)

    total = (keep + exchange(send, "layer", layers, 1).astype(F32)).astype(BF16)
    parts = lax.all_to_all(total, "proc", 0, 0, tiled=True)
    solved_t, parts = lax.optimization_barrier((solved_t, parts))
    total = jnp.sum(parts.reshape(procs, columns, half).astype(F32), axis=0)
    for k in range(1, layers.bit_length() - 1):
        total = total.astype(BF16)
        total = total.astype(F32) + exchange(total, "layer", layers, 1 << k).astype(F32)
    anc_t = lax.dynamic_slice_in_dim(anc_rhs, layer % 2 * half, half, 0).T
    mine = (anc_t - total).astype(BF16)
    ancestor = solve_ancestor(mine, exchange(mine, "layer", layers, 1), anc_inverse).T
    solved = lax.dynamic_slice_in_dim(solved_t, proc * columns, columns, 0).T
    return solved, ancestor


def solution(mesh):
    placed = (
        P("layer", None),
        P(("layer", "proc"), None),
        P(("layer", "proc"), None),
        P(("layer", "proc"), None),
        P(("layer", "proc"), None),
        P(("layer", "proc"), None),
        P(("layer", "proc"), None),
        P(None, "proc"),
        P(),
    )
    return jax.shard_map(
        functools.partial(per_device, mesh.shape["layer"], mesh.shape["proc"]),
        mesh=mesh,
        in_specs=placed,
        out_specs=(P("layer", "proc"), P(None, "proc")),
        check_vma=False,
    )
```
